32 devices in a mesh: cfg: 2 (over x), space: 16 (over z, y, core).
Axes of the slice: x: 2, y: 2, z: 4, core: 2. Of those that a mesh axis runs over, the one named last changes fastest.
Arguments:
- eigenvectors: bfloat16 [8, 2, 3, 128, 16, 1024], P('cfg', None, None, None, 'space'), parts along dimension 0, may hold values from -3 to 3
- link_field: bfloat16 [8, 3, 2, 3, 3, 16, 1024], P('cfg', None, None, None, None, 'space'), parts along dimension 0, may hold values from -2.5 to 2.5
- momentum: int32 [3], replicated, may hold values from -2 to 2
- directions: int32 [4], replicated, may hold values from 0 to 2, as said below
- offsets: int32 [4], replicated, may hold values from 0 to 124
Outputs:
- elementals: float32 [8, 2, 4, 128, 128], P('cfg', None, None, 'space'), parts along dimension 0
The draws below stay inside these ranges and needn't reach their ends.
There are 2 independent parts, one for each index of `cfg`. The reference program is written for one: setup_inputs(seed, part) draws one part's arguments, and reference() takes and returns one part's arrays. A program takes and returns all parts, laid end to end along the dimension named above; an argument that names none is the same for every part. Nothing has to cross between parts.
Inputs may be any that keep to these rules, and one draw needn't show every extreme that they name: `directions`: exactly 2 of the timeslices have direction 0 (the first dimension); each other one has direction 1 or 2.
All inputs are finite; a program needn't handle non-finite values.
Results may differ from the reference program's by a relative error of at most 0.0041.
Values may be sent and summed in bfloat16 or wider, within the bound.
A program may use at most 128 MiB of HBM per device.

```python
import math
import jax
import jax.numpy as jnp
from jax import lax

NEV = 128
BLK = 4
TSL = 4
LY = 32
LZ = 32
LX = 16
LYZ = 1024


def draw_directions(key, part):
    ranking = jax.random.permutation(jax.random.fold_in(key, 17), TSL)
    return jnp.where(ranking < TSL // 2, 0, 1 + ranking % 2).astype(jnp.int32)


def place_ends(values, own_key, least, top_value):
    longest = values.shape.index(max(values.shape))
    spots = []
    for shift in (0, 1):
        where = [jax.random.randint(jax.random.fold_in(own_key, axis), (), 0, length) for axis, length in enumerate(values.shape)]
        where[longest] = (where[longest] + shift) % values.shape[longest]
        spots.append(tuple(where))
    return values.at[spots[0]].set(least).at[spots[1]].set(top_value)


def levels(key, shape, split, least, largest):
    def one(axis_at, parts):
        steps = jax.random.uniform(jax.random.fold_in(jax.random.fold_in(key, 6), axis_at), (parts,), jnp.float32, least / len(split), largest / len(split))
        return jnp.repeat(jnp.exp(steps), shape[axis_at] // parts).reshape((-1,) + (1,) * (len(shape) - axis_at - 1))

    gain = one(*split[0])
    for cut in split[1:]:
        gain = gain * one(*cut)
    return gain


def normal_values(rng, shape, spread, bound, cuts=(), kind=jnp.bfloat16):
    values = spread * jax.random.normal(rng, shape, jnp.float32)
    if cuts:
        values = values * levels(rng, shape, cuts, -0.22, 0.18)
    return jnp.clip(values, -bound, bound).astype(kind)


def setup_inputs(seed: int = 0, part: int = 0) -> dict:
    streams_of = jax.random.split(jax.random.key(seed), 6)
    own_keys = jax.random.split(jax.random.fold_in(streams_of[5], part), 6)
    return {
        "eigenvectors": normal_values(own_keys[0], (TSL, 2, 3, NEV, LX, LYZ), 0.5, 3.0, ((4, 16),)),
        "link_field": normal_values(own_keys[1], (TSL, 3, 2, 3, 3, LX, LYZ), 6 ** -0.5, 2.5, ((5, 16),)),
        "momentum": jax.random.randint(streams_of[2], (3,), -2, 3).astype(jnp.int32),
        "directions": draw_directions(jax.random.fold_in(streams_of[5], 71), part),
        "offsets": place_ends(jax.random.randint(streams_of[4], (TSL,), 0, NEV - BLK + 1), jax.random.fold_in(streams_of[4], 1), 0, NEV - BLK).astype(jnp.int32),
    }


epsilon_cycles = ((0, 1, 2), (1, 2, 0), (2, 0, 1))

def phase_table(momentum, x_sites, extent):
    y_sites = jnp.arange(LY, dtype=jnp.int32)
    z_sites = jnp.arange(LZ, dtype=jnp.int32)
    x_turns = (momentum[0] * x_sites % extent).astype(jnp.float32) / extent
    y_turns = (momentum[1] * y_sites % LY).astype(jnp.float32) / LY
    z_turns = (momentum[2] * z_sites % LZ).astype(jnp.float32) / LZ
    angles = -2.0 * math.pi * (x_turns[:, None, None] + y_turns[None, :, None] + z_turns[None, None, :])
    angles = angles.reshape(x_sites.shape[0], LY * LZ)
    return (jnp.cos(angles), jnp.sin(angles))

def roll_inner(field_in, axis_pos):
    leading_shape = field_in.shape[:-1]
    grid = field_in.reshape(leading_shape + (LY, LZ))
    grid = jnp.roll(grid, -1, axis=axis_pos)
    return grid.reshape(field_in.shape)

def along_first(vectors):
    return jnp.roll(vectors, -1, axis=3)

def along_second(vectors):
    return roll_inner(vectors, -2)

def along_third(vectors):
    return roll_inner(vectors, -1)

def transport(link_now, source):
    link_re = link_now[0].astype(jnp.float32)
    link_im = link_now[1].astype(jnp.float32)
    src_re = source[0].astype(jnp.float32)
    src_im = source[1].astype(jnp.float32)
    rows_re = []
    rows_im = []
    for row in range(3):
        acc_re = link_re[row, 0] * src_re[0] - link_im[row, 0] * src_im[0]
        acc_im = link_re[row, 0] * src_im[0] + link_im[row, 0] * src_re[0]
        for column in range(1, 3):
            acc_re = acc_re + link_re[row, column] * src_re[column] - link_im[row, column] * src_im[column]
            acc_im = acc_im + link_re[row, column] * src_im[column] + link_im[row, column] * src_re[column]
        rows_re.append(acc_re)
        rows_im.append(acc_im)
    return jnp.stack([jnp.stack(rows_re), jnp.stack(rows_im)]).astype(jnp.bfloat16)

def pair_products(leading, partner, cosine, sine_values):
    lead_re = leading[0].astype(jnp.float32)
    lead_im = leading[1].astype(jnp.float32)
    part_re = partner[0].astype(jnp.float32)
    part_im = partner[1].astype(jnp.float32)
    layers = [None, None, None]
    for one_color, two_color, out_color in epsilon_cycles:
        prod_re = lead_re[one_color][:, None] * part_re[two_color][None] - lead_im[one_color][:, None] * part_im[two_color][None] - lead_re[two_color][:, None] * part_re[one_color][None] + lead_im[two_color][:, None] * part_im[one_color][None]
        prod_im = lead_re[one_color][:, None] * part_im[two_color][None] + lead_im[one_color][:, None] * part_re[two_color][None] - lead_re[two_color][:, None] * part_im[one_color][None] - lead_im[two_color][:, None] * part_re[one_color][None]
        layers[out_color] = (prod_re * cosine - prod_im * sine_values, prod_re * sine_values + prod_im * cosine)
    real_part = jnp.stack([layers[0][0], layers[1][0], layers[2][0]])
    imag_part = jnp.stack([layers[0][1], layers[1][1], layers[2][1]])
    return jnp.stack([real_part, imag_part]).astype(jnp.bfloat16)

def contract(products, vectors):
    flat_products = products.reshape(products.shape[:4] + (-1,)).astype(jnp.float32)
    flat_vectors = vectors.reshape(vectors.shape[:3] + (-1,)).astype(jnp.float32)
    blocks = jnp.einsum('rkabs,qkcs->brqac', flat_products, flat_vectors)
    return jnp.stack([blocks[:, 0, 0] - blocks[:, 1, 1], blocks[:, 0, 1] + blocks[:, 1, 0]], axis=1)

def reference(eigenvectors, link_field, momentum, directions, offsets):
    norm_factor = 1.0 / math.sqrt(LX * LY * LZ)
    cos_all, sin_all = phase_table(momentum, jnp.arange(LX, dtype=jnp.int32), LX)
    results = []
    for tslice in range(TSL):
        vectors = eigenvectors[tslice]
        direction = directions[tslice]
        source = lax.switch(direction, [along_first, along_second, along_third], vectors)
        link_now = lax.dynamic_index_in_dim(link_field[tslice], direction, 0, keepdims=False)
        displaced = transport(link_now, source)
        leading = lax.dynamic_slice_in_dim(vectors, offsets[tslice].astype(jnp.int32), BLK, axis=2)

        def accumulate(running, plane, leading=leading, displaced=displaced, vectors=vectors):

            def take_plane(array, axis_pos):
                return lax.dynamic_slice_in_dim(array, plane, 1, axis=axis_pos)
            products = pair_products(take_plane(leading, 3), take_plane(displaced, 3), take_plane(cos_all, 0), take_plane(sin_all, 0))
            return (running + contract(products, take_plane(vectors, 3)), None)
        running, _ = lax.scan(accumulate, jnp.zeros((NEV, 2, BLK, NEV), jnp.float32), jnp.arange(LX, dtype=jnp.int32))
        results.append(jnp.transpose(running * norm_factor, (1, 2, 0, 3)))
    return jnp.stack(results)
```

```python
import functools
import math

import jax
import jax.numpy as jnp
from jax import lax
from jax.experimental import pallas as pl
from jax.experimental.pallas import tpu as pltpu
from jax.sharding import PartitionSpec as P

BLK = 4
LY = 32
LZ = 32
SITES = 256
ROWS = 16
CHUNKS = 2
MESH = pl.DeviceIdType.MESH

epsilon_cycles = ((0, 1, 2), (1, 2, 0), (2, 0, 1))


def phase_table(momentum, x_sites, extent):
    y_sites = jnp.arange(LY, dtype=jnp.int32)
    z_sites = jnp.arange(LZ, dtype=jnp.int32)
    x_turns = (momentum[0] * x_sites % extent).astype(jnp.float32) / extent
    y_turns = (momentum[1] * y_sites % LY).astype(jnp.float32) / LY
    z_turns = (momentum[2] * z_sites % LZ).astype(jnp.float32) / LZ
    angles = (
        -2.0 * math.pi * (x_turns[:, None, None] + y_turns[None, :, None] + z_turns[None, None, :])
    )
    angles = angles.reshape(x_sites.shape[0], LY * LZ)
    return (jnp.cos(angles), jnp.sin(angles))


def products_of(source_at, link_ref, lead_ref, prod_ref, count):
    def rows_step(step, carry):
        first = pl.multiple_of(step * ROWS, ROWS)
        src_re = [source_at(0, c, first) for c in range(3)]
        src_im = [source_at(1, c, first) for c in range(3)]
        part_re = []
        part_im = []
        for row in range(3):
            acc_re = None
            acc_im = None
            for column in range(3):
                link_re = link_ref[0, row * 3 + column][None]
                link_im = link_ref[0, 9 + row * 3 + column][None]
                now_re = link_re * src_re[column] - link_im * src_im[column]
                now_im = link_re * src_im[column] + link_im * src_re[column]
                acc_re = now_re if acc_re is None else acc_re + now_re
                acc_im = now_im if acc_im is None else acc_im + now_im
            part_re.append(acc_re.astype(jnp.bfloat16).astype(jnp.float32))
            part_im.append(acc_im.astype(jnp.bfloat16).astype(jnp.float32))
        for a in range(BLK):
            lead_re = [lead_ref[0, c * BLK + a][None] for c in range(3)]
            lead_im = [lead_ref[0, (3 + c) * BLK + a][None] for c in range(3)]
            for one, two, out in epsilon_cycles:
                prod_re = (
                    lead_re[one] * part_re[two]
                    - lead_im[one] * part_im[two]
                    - lead_re[two] * part_re[one]
                    + lead_im[two] * part_im[one]
                )
                prod_im = (
                    lead_re[one] * part_im[two]
                    + lead_im[one] * part_re[two]
                    - lead_re[two] * part_im[one]
                    - lead_im[two] * part_re[one]
                )
                where = pl.ds(out * SITES, SITES)
                at_re = pl.multiple_of(a * count + first, ROWS)
                at_im = pl.multiple_of((BLK + a) * count + first, ROWS)
                prod_ref[pl.ds(at_re, ROWS), where] = prod_re.astype(jnp.bfloat16)
                prod_ref[pl.ds(at_im, ROWS), where] = prod_im.astype(jnp.bfloat16)
        return carry

    lax.fori_loop(0, count // ROWS, rows_step, 0)


def add_sites(vectors_ref, prod_ref, acc_ref, step):
    nev = vectors_ref.shape[3]
    total = None
    for k in range(3):
        weights = vectors_ref[0, :, k].reshape(2 * nev, SITES)
        now = lax.dot_general(
            prod_ref[:, k * SITES : (k + 1) * SITES],
            weights,
            (((1,), (1,)), ((), ())),
            preferred_element_type=jnp.float32,
        )
        total = now if total is None else total + now

    @pl.when(step == 0)
    def _():
        acc_ref[...] = total

    @pl.when(step > 0)
    def _():
        acc_ref[...] += total


def write_out(acc_ref, out_ref, count, nev, norm_factor, lead_index):
    half = BLK * count
    for a in range(BLK):
        rows_re = acc_ref[a * count : (a + 1) * count]
        rows_im = acc_ref[half + a * count : half + (a + 1) * count]
        out_re = (rows_re[:, :nev] - rows_im[:, nev:]) * norm_factor
        out_im = (rows_re[:, nev:] + rows_im[:, :nev]) * norm_factor
        for g in range(count // 8):
            out_ref[lead_index + (g, a)] = out_re[g * 8 : g * 8 + 8]
            out_ref[lead_index + (g, BLK + a)] = out_im[g * 8 : g * 8 + 8]


def local_kernel(norm_factor, info, vec_ref, next_ref, link_ref, lead_ref, out_ref, src_ref, prod_ref, acc_ref):
    step = pl.program_id(1)
    nev = vec_ref.shape[3]
    direction = info[2 + pl.program_id(0)]
    lane = lax.broadcasted_iota(jnp.int32, (ROWS, SITES), 1)

    def shift(second):
        def rows_step(i, carry):
            rows = pl.ds(pl.multiple_of(i * ROWS, ROWS), ROWS)
            for r in range(2):
                for c in range(3):
                    now = vec_ref[0, r, c, rows].astype(jnp.float32)
                    if second:
                        after = next_ref[0, r, c, rows].astype(jnp.float32)
                        moved = jnp.where(
                            lane < SITES - LZ,
                            pltpu.roll(now, SITES - LZ, 1),
                            pltpu.roll(after, SITES - LZ, 1),
                        )
                    else:
                        moved = jnp.where(
                            lane % LZ == LZ - 1,
                            pltpu.roll(now, LZ - 1, 1),
                            pltpu.roll(now, SITES - 1, 1),
                        )
                    src_ref[r, c, rows] = moved
            return carry

        lax.fori_loop(0, nev // ROWS, rows_step, 0)

    @pl.when(direction == 1)
    def _():
        shift(True)

    @pl.when(direction != 1)
    def _():
        shift(False)

    products_of(lambda r, c, first: src_ref[r, c, pl.ds(first, ROWS)], link_ref, lead_ref, prod_ref, nev)
    add_sites(vec_ref, prod_ref, acc_ref, step)

    @pl.when(step == pl.num_programs(1) - 1)
    def _():
        write_out(acc_ref, out_ref, nev, nev, norm_factor, (0,))


def remote_kernel(norm_factor, info, vec_ref, src_ref, link_ref, lead_ref, out_ref, prod_ref, acc_ref):
    step = pl.program_id(0)
    nev = vec_ref.shape[3]
    count = src_ref.shape[2]
    products_of(
        lambda r, c, first: src_ref[r, c, pl.ds(first, ROWS)].astype(jnp.float32),
        link_ref, lead_ref, prod_ref, count,
    )
    add_sites(vec_ref, prod_ref, acc_ref, step)

    @pl.when(step == pl.num_programs(0) - 1)
    def _():
        write_out(acc_ref, out_ref, count, nev, norm_factor, ())


def local_sums(info, vectors, links, leads, norm_factor):
    slices, _, _, nev, sites = vectors.shape
    steps = sites // SITES
    count = slices // 2
    flops = count * 2 * 8 * nev * 3 * sites * 2 * nev
    return pl.pallas_call(
        functools.partial(local_kernel, norm_factor),
        out_shape=jax.ShapeDtypeStruct((count, nev // 8, 2 * BLK, 8, nev), jnp.float32),
        grid_spec=pltpu.PrefetchScalarGridSpec(
            num_scalar_prefetch=1,
            grid=(count, steps),
            in_specs=[
                pl.BlockSpec((1, 2, 3, nev, SITES), lambda t, s, info: (info[t], 0, 0, 0, s)),
                pl.BlockSpec((1, 2, 3, nev, SITES), lambda t, s, info: (info[t], 0, 0, 0, (s + 1) % steps)),
                pl.BlockSpec((1, 18, SITES), lambda t, s, info: (count + t, 0, s)),
                pl.BlockSpec((1, 6 * BLK, SITES), lambda t, s, info: (count + t, 0, s)),
            ],
            out_specs=pl.BlockSpec((1, nev // 8, 2 * BLK, 8, nev), lambda t, s, info: (t, 0, 0, 0, 0)),
            scratch_shapes=[
                pltpu.VMEM((2, 3, nev, SITES), jnp.float32),
                pltpu.VMEM((2 * BLK * nev, 3 * SITES), jnp.bfloat16),
                pltpu.VMEM((2 * BLK * nev, 2 * nev), jnp.float32),
            ],
        ),
        compiler_params=pltpu.CompilerParams(vmem_limit_bytes=40 * 2**20),
        cost_estimate=pl.CostEstimate(flops=flops, bytes_accessed=count * 4 * 2**20, transcendentals=0),
        name="local_sums",
    )(info, vectors, vectors, links, leads)


def remote_sums(info, vectors, source, links, leads, place, norm_factor):
    _, _, _, nev, sites = vectors.shape
    count = source.shape[2]
    steps = sites // SITES
    flops = 2 * 8 * count * 3 * sites * 2 * nev
    return pl.pallas_call(
        functools.partial(remote_kernel, norm_factor),
        out_shape=jax.ShapeDtypeStruct((count // 8, 2 * BLK, 8, nev), jnp.float32),
        grid_spec=pltpu.PrefetchScalarGridSpec(
            num_scalar_prefetch=1,
            grid=(steps,),
            in_specs=[
                pl.BlockSpec((1, 2, 3, nev, SITES), lambda s, info: (info[0], 0, 0, 0, s)),
                pl.BlockSpec((2, 3, count, SITES), lambda s, info: (0, 0, 0, s)),
                pl.BlockSpec((1, 18, SITES), lambda s, info: (place, 0, s)),
                pl.BlockSpec((1, 6 * BLK, SITES), lambda s, info: (place, 0, s)),
            ],
            out_specs=pl.BlockSpec((count // 8, 2 * BLK, 8, nev), lambda s, info: (0, 0, 0, 0)),
            scratch_shapes=[
                pltpu.VMEM((2 * BLK * count, 3 * SITES), jnp.bfloat16),
                pltpu.VMEM((2 * BLK * count, 2 * nev), jnp.float32),
            ],
        ),
        compiler_params=pltpu.CompilerParams(vmem_limit_bytes=40 * 2**20),
        cost_estimate=pl.CostEstimate(flops=flops, bytes_accessed=3 * 2**20, transcendentals=0),
        name="remote_sums",
    )(info, vectors, source, links, leads)


def scatter_kernel(groups, part_ref, out_ref, send_one, send_two, send_three, recv_one, recv_two, recv_three, sum_one, sum_two, sems_out, sems_in):
    me = lax.axis_index("space")
    core = me % 2
    row = (me // 2) % 2
    group = me // 4
    pair = me + 1 - 2 * core
    across = me + 2 - 4 * row
    others = [(group + step) % groups for step in range(1, groups)]
    barrier = pltpu.get_barrier_semaphore()
    for partner in [pair, across] + [other * 4 + row * 2 + core for other in others]:
        pl.semaphore_signal(barrier, inc=1, device_id={"space": partner}, device_id_type=MESH)
    pl.semaphore_wait(barrier, groups + 1)

    def copy(source, target, number, partner):
        return pltpu.make_async_remote_copy(
            src_ref=source, dst_ref=target, send_sem=sems_out.at[number], recv_sem=sems_in.at[number],
            device_id={"space": partner}, device_id_type=MESH,
        )

    for z in range(groups):
        for y in range(2):
            send_one[z, y] = part_ref[z, y, 1 - core].astype(jnp.bfloat16)
    first = copy(send_one, recv_one, 0, pair)
    first.start()
    first.wait()
    for z in range(groups):
        got = part_ref[z, 1 - row, core] + recv_one[z, 1 - row].astype(jnp.float32)
        send_two[z] = got.astype(jnp.bfloat16)
    second = copy(send_two, recv_two, 1, across)
    second.start()
    for z in range(groups):
        sum_one[z] = part_ref[z, row, core] + recv_one[z, row].astype(jnp.float32)
    second.wait()
    for z in range(groups):
        sum_two[z] = sum_one[z] + recv_two[z].astype(jnp.float32)
        send_three[z] = sum_two[z].astype(jnp.bfloat16)
    copies = []
    for step, other in enumerate(others):
        copies.append(copy(send_three.at[other], recv_three.at[step], 2 + step, other * 4 + row * 2 + core))
        copies[-1].start()
    total = sum_two[group]
    for step in range(groups - 1):
        copies[step].wait()
        total = total + recv_three[step].astype(jnp.float32)
    out_ref[...] = total


def scatter_sum(part, number):
    devices, rows, columns = part.shape
    groups = devices // 4
    whole = pl.BlockSpec(memory_space=pltpu.VMEM)
    bf16 = jnp.bfloat16
    return pl.pallas_call(
        functools.partial(scatter_kernel, groups),
        out_shape=jax.ShapeDtypeStruct((rows, columns), jnp.float32),
        in_specs=[whole],
        out_specs=whole,
        scratch_shapes=[
            pltpu.VMEM((groups, 2, rows, columns), bf16),
            pltpu.VMEM((groups, rows, columns), bf16),
            pltpu.VMEM((groups, rows, columns), bf16),
            pltpu.VMEM((groups, 2, rows, columns), bf16),
            pltpu.VMEM((groups, rows, columns), bf16),
            pltpu.VMEM((groups, rows, columns), bf16),
            pltpu.VMEM((groups, rows, columns), jnp.float32),
            pltpu.VMEM((groups, rows, columns), jnp.float32),
            pltpu.SemaphoreType.DMA((groups + 1,)),
            pltpu.SemaphoreType.DMA((groups + 1,)),
        ],
        compiler_params=pltpu.CompilerParams(
            collective_id=number, has_side_effects=True, vmem_limit_bytes=40 * 2**20
        ),
        name="scatter_sum",
    )(part.reshape(groups, 2, 2, rows, columns))


def by_owner(part, devices):
    slices, tiles, parts, eight, nev = part.shape
    own = tiles * eight // devices
    if own == eight:
        moved = jnp.transpose(part, (1, 0, 2, 3, 4))
    else:
        flat = jnp.transpose(part, (0, 2, 1, 3, 4)).reshape(slices, parts, devices, own, nev)
        moved = jnp.transpose(flat, (2, 0, 1, 3, 4))
    return moved.reshape(devices, slices * parts * own, nev)


def on_device(eigenvectors, link_field, momentum, directions, offsets):
    devices = lax.axis_size("space")
    slices, _, _, nev, planes, sites = eigenvectors.shape
    extent_x = planes * devices
    norm_factor = 1.0 / math.sqrt(extent_x * LY * LZ)
    x_sites = lax.axis_index("space") * planes + jnp.arange(planes, dtype=jnp.int32)
    vectors = eigenvectors.reshape(slices, 2, 3, nev, sites)

    inner = (directions != 0).astype(jnp.int32)
    numbers = jnp.arange(slices, dtype=jnp.int32)
    before = (inner[None] < inner[:, None]) | (
        (inner[None] == inner[:, None]) & (numbers[None] < numbers[:, None])
    )
    rank = jnp.sum(before.astype(jnp.int32), axis=1)
    order = [jnp.sum(jnp.where(rank == place, numbers, 0)) for place in range(slices)]
    half = slices // 2

    size = nev // CHUNKS
    pairs = [(source, (source - 1) % devices) for source in range(devices)]
    above = []
    for place in range(half):
        for chunk in range(CHUNKS):
            piece = lax.dynamic_slice(
                vectors, (order[place], 0, 0, chunk * size, 0), (1, 2, 3, size, sites)
            )
            above.append(lax.ppermute(piece, "space", pairs)[0])

    cosine, sine = phase_table(momentum, x_sites, extent_x)
    links = []
    leads = []
    for place in range(slices):
        now = order[place]
        link = lax.dynamic_slice(
            link_field, (now, directions[now], 0, 0, 0, 0, 0), (1, 1) + link_field.shape[2:]
        )
        links.append(link.reshape(18, sites).astype(jnp.float32))
        lead = lax.dynamic_slice(
            vectors, (now, 0, 0, offsets[now], 0), (1, 2, 3, BLK, sites)
        )[0].astype(jnp.float32)
        turned = jnp.stack([lead[0] * cosine - lead[1] * sine, lead[0] * sine + lead[1] * cosine])
        leads.append(turned.reshape(6 * BLK, sites))
    links = jnp.stack(links)
    leads = jnp.stack(leads)

    info = jnp.stack(order[half:] + [directions[now] for now in order[half:]])
    inner_part = local_sums(info, vectors, links, leads, norm_factor)
    inner_sum = scatter_sum(by_owner(inner_part, devices), 0)
    outer = []
    for place in range(half):
        pieces = [
            remote_sums(
                order[place][None], vectors, above[place * CHUNKS + chunk], links, leads, place, norm_factor
            )
            for chunk in range(CHUNKS)
        ]
        outer.append(jnp.concatenate(pieces))
    outer_sum = scatter_sum(by_owner(jnp.stack(outer), devices), 1)

    own = nev // devices
    both = jnp.concatenate([outer_sum, inner_sum]).reshape(slices, 2, BLK, own, nev)
    return jnp.take(both, rank, axis=0, mode="clip")


def solution(mesh):
    placed = (
        P("cfg", None, None, None, "space", None),
        P("cfg", None, None, None, None, "space", None),
        P(),
        P(),
        P(),
    )
    return jax.shard_map(
        on_device,
        mesh=mesh,
        in_specs=placed,
        out_specs=P("cfg", None, None, "space", None),
        check_vma=False,
    )
```

```python
import functools
import math

import jax
import jax.numpy as jnp
from jax import lax
from jax.experimental import pallas as pl
from jax.experimental.pallas import tpu as pltpu
from jax.sharding import PartitionSpec as P

BLK = 4
LY = 32
LZ = 32
SITES = 256
ROWS = 16
CHUNKS = 2
MESH = pl.DeviceIdType.MESH

epsilon_cycles = ((0, 1, 2), (1, 2, 0), (2, 0, 1))


def phase_row(momentum, x_site, extent, sites):
    site = lax.broadcasted_iota(jnp.int32, (1, sites), 1)
    x_turn = lax.rem(lax.rem(momentum[0] * x_site, extent) + extent, extent)
    y_turns = lax.rem(lax.rem(momentum[1] * (site // LZ), LY) + LY, LY).astype(jnp.float32) / LY
    z_turns = lax.rem(lax.rem(momentum[2] * (site % LZ), LZ) + LZ, LZ).astype(jnp.float32) / LZ
    angles = -2.0 * math.pi * (x_turn.astype(jnp.float32) / extent + y_turns + z_turns)
    return jnp.cos(angles), jnp.sin(angles)


def stage_rows(extent, offset, momentum, vec_ref, link_ref, wide_ref, link_rows, lead_rows, weights):
    nev, sites = vec_ref.shape[3:]
    for row in range(3):
        for column in range(3):
            at = 2 * (3 * row + column)
            link_rows[at : at + 2] = link_ref[0, 0, row, column].astype(jnp.float32)
    cosine, sine = phase_row(momentum, lax.axis_index("space"), extent, sites)
    base = pl.multiple_of(jnp.minimum((offset // 16) * 16, nev - 32), 16)
    for c in range(3):
        for r in range(2):
            wide_ref[r] = vec_ref[0, r, c, pl.ds(base, 32)].astype(jnp.float32)
        for a in range(BLK):
            now_re = wide_ref[0, pl.ds(offset - base + a, 1)]
            now_im = wide_ref[1, pl.ds(offset - base + a, 1)]
            at = 2 * (c * BLK + a)
            lead_rows[at : at + 1] = now_re * cosine - now_im * sine
            lead_rows[at + 1 : at + 2] = now_re * sine + now_im * cosine
    for part in range(sites // SITES):
        for r in range(2):
            for k in range(3):
                weights[part, r * nev : (r + 1) * nev, k * SITES : (k + 1) * SITES] = vec_ref[
                    0, r, k, :, part * SITES : (part + 1) * SITES
                ]


def dot_rows(left, right):
    return lax.dot_general(left, right, (((1,), (1,)), ((), ())), preferred_element_type=jnp.float32)


def sums_of(source_at, count, sites, link_rows, lead_rows, weights, prods, acc_ref):
    share = 2 * BLK * ROWS

    for part in range(sites // SITES):
        lanes = slice(part * SITES, (part + 1) * SITES)
        prod_ref = prods[part % 2]
        last_ref = prods[(part + 1) % 2]

        def rows_step(step, carry, part=part, lanes=lanes, prod_ref=prod_ref, last_ref=last_ref):
            if part > 0:
                rows = pl.ds(pl.multiple_of(step * share, share), share)
                now = dot_rows(last_ref[rows], weights[part - 1])
                acc_ref[rows] = now if part == 1 else acc_ref[rows] + now
            first = pl.multiple_of(step * ROWS, ROWS)
            src_re = [source_at(0, c, first, lanes) for c in range(3)]
            src_im = [source_at(1, c, first, lanes) for c in range(3)]
            part_re = []
            part_im = []
            for row in range(3):
                acc_re = None
                acc_im = None
                for column in range(3):
                    at = 2 * (row * 3 + column)
                    link_re = link_rows[at : at + 1, lanes]
                    link_im = link_rows[at + 1 : at + 2, lanes]
                    now_re = link_re * src_re[column] - link_im * src_im[column]
                    now_im = link_re * src_im[column] + link_im * src_re[column]
                    acc_re = now_re if acc_re is None else acc_re + now_re
                    acc_im = now_im if acc_im is None else acc_im + now_im
                part_re.append(acc_re.astype(jnp.bfloat16).astype(jnp.float32))
                part_im.append(acc_im.astype(jnp.bfloat16).astype(jnp.float32))
            for a in range(BLK):
                lead_re = []
                lead_im = []
                for c in range(3):
                    at = 2 * (c * BLK + a)
                    lead_re.append(lead_rows[at : at + 1, lanes])
                    lead_im.append(lead_rows[at + 1 : at + 2, lanes])
                for one, two, out in epsilon_cycles:
                    prod_re = (
                        lead_re[one] * part_re[two]
                        - lead_im[one] * part_im[two]
                        - lead_re[two] * part_re[one]
                        + lead_im[two] * part_im[one]
                    )
                    prod_im = (
                        lead_re[one] * part_im[two]
                        + lead_im[one] * part_re[two]
                        - lead_re[two] * part_im[one]
                        - lead_im[two] * part_re[one]
                    )
                    where = slice(out * SITES, (out + 1) * SITES)
                    at_re = pl.multiple_of(a * count + first, ROWS)
                    at_im = pl.multiple_of((BLK + a) * count + first, ROWS)
                    prod_ref[pl.ds(at_re, ROWS), where] = prod_re.astype(jnp.bfloat16)
                    prod_ref[pl.ds(at_im, ROWS), where] = prod_im.astype(jnp.bfloat16)
            return carry

        lax.fori_loop(0, count // ROWS, rows_step, 0)


def write_out(acc_ref, last_ref, last_weights, out_ref, count, nev, norm_factor):
    half = BLK * count
    for a in range(BLK):
        at_re = slice(a * count, (a + 1) * count)
        at_im = slice(half + a * count, half + (a + 1) * count)
        rows_re = acc_ref[at_re] + dot_rows(last_ref[at_re], last_weights[...])
        rows_im = acc_ref[at_im] + dot_rows(last_ref[at_im], last_weights[...])
        out_re = (rows_re[:, :nev] - rows_im[:, nev:]) * norm_factor
        out_im = (rows_re[:, nev:] + rows_im[:, :nev]) * norm_factor
        for g in range(count // 8):
            out_ref[g, a] = out_re[g * 8 : g * 8 + 8]
            out_ref[g, BLK + a] = out_im[g * 8 : g * 8 + 8]


def shift_sources(second, vec_ref, src_ref):
    nev, sites = vec_ref.shape[3:]
    lane = lax.broadcasted_iota(jnp.int32, (ROWS, sites), 1)

    def rows_step(i, carry):
        rows = pl.ds(pl.multiple_of(i * ROWS, ROWS), ROWS)
        for r in range(2):
            for c in range(3):
                now = vec_ref[0, r, c, rows].astype(jnp.float32)
                if second:
                    moved = pltpu.roll(now, sites - LZ, 1)
                else:
                    moved = jnp.where(
                        lane % LZ == LZ - 1,
                        pltpu.roll(now, LZ - 1, 1),
                        pltpu.roll(now, sites - 1, 1),
                    )
                src_ref[r, c, rows] = moved
        return carry

    lax.fori_loop(0, nev // ROWS, rows_step, 0)


def sums_kernel(place, extent, norm_factor, order, directions, offsets, momentum, vec_ref, link_ref, *refs):
    nev, sites = vec_ref.shape[3:]
    now = order[place]
    if len(refs) == 9:
        src_ref, out_ref, wide_ref, link_rows, lead_rows, weights, prod_a, prod_b, acc_ref = refs
        count = src_ref.shape[2]

        def source_at(r, c, first, lanes):
            return src_ref[r, c, pl.ds(first, ROWS), lanes].astype(jnp.float32)
    else:
        out_ref, wide_ref, link_rows, lead_rows, weights, prod_a, prod_b, acc_ref, moved_ref, _ = refs
        count = nev

        def source_at(r, c, first, lanes):
            return moved_ref[r, c, pl.ds(first, ROWS), lanes]

        @pl.when(directions[now] == 1)
        def _():
            shift_sources(True, vec_ref, moved_ref)

        @pl.when(directions[now] != 1)
        def _():
            shift_sources(False, vec_ref, moved_ref)

    stage_rows(extent, offsets[now], momentum, vec_ref, link_ref, wide_ref, link_rows, lead_rows, weights)
    sums_of(source_at, count, sites, link_rows, lead_rows, weights, (prod_a, prod_b), acc_ref)
    parts = sites // SITES
    write_out(acc_ref, (prod_a, prod_b)[(parts - 1) % 2], weights.at[parts - 1], out_ref, count, nev, norm_factor)


def slice_sums(scalars, vectors, links, source, place, extent, norm_factor):
    _, _, _, nev, sites = vectors.shape
    parts = sites // SITES
    count = nev if source is None else source.shape[2]
    operands = [vectors, links] + ([] if source is None else [source])
    in_specs = [
        pl.BlockSpec((1, 2, 3, nev, sites), lambda i, order, *_: (order[place], 0, 0, 0, 0)),
        pl.BlockSpec(
            (1, 1, 3, 3, 2, sites),
            lambda i, order, directions, *_: (order[place], directions[order[place]], 0, 0, 0, 0),
        ),
    ]
    scratch = [
        pltpu.VMEM((2, 32, sites), jnp.float32),
        pltpu.VMEM((18, sites), jnp.float32),
        pltpu.VMEM((6 * BLK, sites), jnp.float32),
        pltpu.VMEM((parts, 2 * nev, 3 * SITES), jnp.bfloat16),
        pltpu.VMEM((2 * BLK * count, 3 * SITES), jnp.bfloat16),
        pltpu.VMEM((2 * BLK * count, 3 * SITES), jnp.bfloat16),
        pltpu.VMEM((2 * BLK * count, 2 * nev), jnp.float32),
    ]
    if source is None:
        scratch += [pltpu.VMEM((2, 3, nev, sites), jnp.float32), pltpu.VMEM((8, 128), jnp.float32)]
    else:
        in_specs.append(pl.BlockSpec((2, 3, count, sites), lambda i, *_: (0, 0, 0, 0)))
    return pl.pallas_call(
        functools.partial(sums_kernel, place, extent, norm_factor),
        out_shape=jax.ShapeDtypeStruct((count // 8, 2 * BLK, 8, nev), jnp.float32),
        grid_spec=pltpu.PrefetchScalarGridSpec(
            num_scalar_prefetch=4,
            grid=(1,),
            in_specs=in_specs,
            out_specs=pl.BlockSpec((count // 8, 2 * BLK, 8, nev), lambda i, *_: (0, 0, 0, 0)),
            scratch_shapes=scratch,
        ),
        compiler_params=pltpu.CompilerParams(vmem_limit_bytes=40 * 2**20),
        cost_estimate=pl.CostEstimate(
            flops=100 * 2 * BLK * count * 3 * sites, bytes_accessed=2 * 2**20, transcendentals=0
        ),
        name="inner_sums" if source is None else "outer_sums",
    )(*scalars, *operands)


def scatter_kernel(groups, part_ref, out_ref, send_one, send_two, send_three, recv_one, recv_two, recv_three, sum_one, sum_two, sems_out, sems_in):
    me = lax.axis_index("space")
    core = me % 2
    row = (me // 2) % 2
    group = me // 4
    pair = me + 1 - 2 * core
    across = me + 2 - 4 * row
    others = [(group + step) % groups for step in range(1, groups)]
    barrier = pltpu.get_barrier_semaphore()
    for partner in [pair, across] + [other * 4 + row * 2 + core for other in others]:
        pl.semaphore_signal(barrier, inc=1, device_id={"space": partner}, device_id_type=MESH)
    pl.semaphore_wait(barrier, groups + 1)

    def copy(source, target, number, partner):
        return pltpu.make_async_remote_copy(
            src_ref=source, dst_ref=target, send_sem=sems_out.at[number], recv_sem=sems_in.at[number],
            device_id={"space": partner}, device_id_type=MESH,
        )

    for z in range(groups):
        for y in range(2):
            send_one[z, y] = part_ref[z, y, 1 - core].astype(jnp.bfloat16)
    first = copy(send_one, recv_one, 0, pair)
    first.start()
    first.wait()
    for z in range(groups):
        got = part_ref[z, 1 - row, core] + recv_one[z, 1 - row].astype(jnp.float32)
        send_two[z] = got.astype(jnp.bfloat16)
    second = copy(send_two, recv_two, 1, across)
    second.start()
    for z in range(groups):
        sum_one[z] = part_ref[z, row, core] + recv_one[z, row].astype(jnp.float32)
    second.wait()
    for z in range(groups):
        sum_two[z] = sum_one[z] + recv_two[z].astype(jnp.float32)
        send_three[z] = sum_two[z].astype(jnp.bfloat16)
    copies = []
    for step, other in enumerate(others):
        copies.append(copy(send_three.at[other], recv_three.at[step], 2 + step, other * 4 + row * 2 + core))
        copies[-1].start()
    total = sum_two[group]
    for step in range(groups - 1):
        copies[step].wait()
        total = total + recv_three[step].astype(jnp.float32)
    out_ref[...] = total


def scatter_sum(part, number):
    devices, rows, columns = part.shape
    groups = devices // 4
    whole = pl.BlockSpec(memory_space=pltpu.VMEM)
    bf16 = jnp.bfloat16
    return pl.pallas_call(
        functools.partial(scatter_kernel, groups),
        out_shape=jax.ShapeDtypeStruct((rows, columns), jnp.float32),
        in_specs=[whole],
        out_specs=whole,
        scratch_shapes=[
            pltpu.VMEM((groups, 2, rows, columns), bf16),
            pltpu.VMEM((groups, rows, columns), bf16),
            pltpu.VMEM((groups, rows, columns), bf16),
            pltpu.VMEM((groups, 2, rows, columns), bf16),
            pltpu.VMEM((groups, rows, columns), bf16),
            pltpu.VMEM((groups, rows, columns), bf16),
            pltpu.VMEM((groups, rows, columns), jnp.float32),
            pltpu.VMEM((groups, rows, columns), jnp.float32),
            pltpu.SemaphoreType.DMA((groups + 1,)),
            pltpu.SemaphoreType.DMA((groups + 1,)),
        ],
        compiler_params=pltpu.CompilerParams(
            collective_id=number, has_side_effects=True, vmem_limit_bytes=40 * 2**20
        ),
        name="scatter_sum",
    )(part.reshape(groups, 2, 2, rows, columns))


def by_owner(part, devices):
    slices, tiles, parts, eight, nev = part.shape
    own = tiles * eight // devices
    if own == eight:
        moved = jnp.transpose(part, (1, 0, 2, 3, 4))
    else:
        flat = jnp.transpose(part, (0, 2, 1, 3, 4)).reshape(slices, parts, devices, own, nev)
        moved = jnp.transpose(flat, (2, 0, 1, 3, 4))
    return moved.reshape(devices, slices * parts * own, nev)


def on_device(eigenvectors, link_field, momentum, directions, offsets):
    devices = lax.axis_size("space")
    slices, _, _, nev, planes, sites = eigenvectors.shape
    extent_x = planes * devices
    norm_factor = 1.0 / math.sqrt(extent_x * LY * LZ)
    vectors = eigenvectors.reshape(slices, 2, 3, nev, sites)

    inner = (directions != 0).astype(jnp.int32)
    numbers = jnp.arange(slices, dtype=jnp.int32)
    before = (inner[None] < inner[:, None]) | (
        (inner[None] == inner[:, None]) & (numbers[None] < numbers[:, None])
    )
    rank = jnp.sum(before.astype(jnp.int32), axis=1)
    order = [jnp.sum(jnp.where(rank == place, numbers, 0)) for place in range(slices)]
    half = slices // 2

    size = nev // CHUNKS
    pairs = [(source, (source - 1) % devices) for source in range(devices)]
    above = []
    for place in range(half):
        for chunk in range(CHUNKS):
            piece = lax.dynamic_slice(
                vectors, (order[place], 0, 0, chunk * size, 0), (1, 2, 3, size, sites)
            )
            above.append(lax.ppermute(piece, "space", pairs)[0])

    links = jnp.transpose(
        link_field.reshape(slices, 3, 2, 3, 3, sites), (0, 1, 3, 4, 2, 5)
    )
    scalars = (jnp.stack(order), directions, offsets, momentum)
    sums_at = functools.partial(slice_sums, scalars, vectors, links, extent=extent_x, norm_factor=norm_factor)
    results = [None] * slices
    for place in range(half, slices):
        part = by_owner(sums_at(None, place)[None], devices)
        results[place] = lax.psum_scatter(part, "space", scatter_dimension=0, tiled=True)
    for place in range(half):
        pieces = [sums_at(above[place * CHUNKS + chunk], place) for chunk in range(CHUNKS)]
        part = by_owner(jnp.concatenate(pieces)[None], devices)
        if place < half - 1:
            results[place] = lax.psum_scatter(part, "space", scatter_dimension=0, tiled=True)
        else:
            results[place] = scatter_sum(part, 0)[None]

    own = nev // devices
    both = jnp.concatenate(results).reshape(slices, 2, BLK, own, nev)
    return jnp.take(both, rank, axis=0, mode="clip")


def solution(mesh):
    placed = (
        P("cfg", None, None, None, "space", None),
        P("cfg", None, None, None, None, "space", None),
        P(),
        P(),
        P(),
    )
    return jax.shard_map(
        on_device,
        mesh=mesh,
        in_specs=placed,
        out_specs=P("cfg", None, None, "space", None),
        check_vma=False,
    )
```

```python
import functools
import math

import jax
import jax.numpy as jnp
from jax import lax
from jax.experimental import pallas as pl
from jax.experimental.pallas import tpu as pltpu
from jax.sharding import PartitionSpec as P

BLK = 4
LY = 32
LZ = 32
SITES = 256
ROWS = 16
MESH = pl.DeviceIdType.MESH

epsilon_cycles = ((0, 1, 2), (1, 2, 0), (2, 0, 1))


def phase_row(momentum, x_site, extent, sites):
    site = lax.broadcasted_iota(jnp.int32, (1, sites), 1)
    x_turn = lax.rem(lax.rem(momentum[0] * x_site, extent) + extent, extent)
    y_turns = lax.rem(lax.rem(momentum[1] * (site // LZ), LY) + LY, LY).astype(jnp.float32) / LY
    z_turns = lax.rem(lax.rem(momentum[2] * (site % LZ), LZ) + LZ, LZ).astype(jnp.float32) / LZ
    angles = -2.0 * math.pi * (x_turn.astype(jnp.float32) / extent + y_turns + z_turns)
    return jnp.cos(angles), jnp.sin(angles)


def stage_rows(extent, offset, momentum, vec_ref, link_ref, wide_ref, link_rows, lead_rows, weights):
    nev, sites = vec_ref.shape[3:]
    for row in range(3):
        for column in range(3):
            at = 3 * (3 * row + column)
            pair = link_ref[0, 0, row, column].astype(jnp.float32)
            link_rows[at : at + 1] = pair[0:1]
            link_rows[at + 1 : at + 2] = pair[0:1] + pair[1:2]
            link_rows[at + 2 : at + 3] = pair[1:2] - pair[0:1]
    cosine, sine = phase_row(momentum, lax.axis_index("space"), extent, sites)
    base = pl.multiple_of(jnp.minimum((offset // 16) * 16, nev - 32), 16)
    for c in range(3):
        for r in range(2):
            wide_ref[r] = vec_ref[0, r, c, pl.ds(base, 32)].astype(jnp.float32)
        for a in range(BLK):
            now_re = wide_ref[0, pl.ds(offset - base + a, 1)]
            now_im = wide_ref[1, pl.ds(offset - base + a, 1)]
            at = 3 * (c * BLK + a)
            turned_re = now_re * cosine - now_im * sine
            turned_im = now_re * sine + now_im * cosine
            lead_rows[at : at + 1] = turned_re
            lead_rows[at + 1 : at + 2] = turned_re + turned_im
            lead_rows[at + 2 : at + 3] = turned_im - turned_re
    for part in range(sites // SITES):
        for r in range(2):
            for k in range(3):
                weights[part, r * nev : (r + 1) * nev, k * SITES : (k + 1) * SITES] = vec_ref[
                    0, r, k, :, part * SITES : (part + 1) * SITES
                ]


def sum_of(terms):
    return functools.reduce(lambda left, right: left + right, terms)


def dot_rows(left, right):
    return lax.dot_general(left, right, (((1,), (1,)), ((), ())), preferred_element_type=jnp.float32)


def sums_of(source_at, count, sites, link_rows, lead_rows, weights, prods, acc_ref):
    share = 2 * BLK * ROWS

    for part in range(sites // SITES):
        lanes = slice(part * SITES, (part + 1) * SITES)
        prod_ref = prods[part % 2]
        last_ref = prods[(part + 1) % 2]

        def rows_step(step, carry, part=part, lanes=lanes, prod_ref=prod_ref, last_ref=last_ref):
            if part > 0:
                rows = pl.ds(pl.multiple_of(step * share, share), share)
                now = dot_rows(last_ref[rows], weights[part - 1])
                acc_ref[rows] = now if part == 1 else acc_ref[rows] + now
            first = pl.multiple_of(step * ROWS, ROWS)
            src_re = [source_at(0, c, first, lanes) for c in range(3)]
            src_im = [source_at(1, c, first, lanes) for c in range(3)]
            src_sum = [src_re[c] + src_im[c] for c in range(3)]
            part_re = []
            part_im = []
            for row in range(3):
                rows_now = [
                    [link_rows[at + n : at + n + 1, lanes] for n in range(3)]
                    for at in (9 * row, 9 * row + 3, 9 * row + 6)
                ]
                common = sum_of(rows_now[c][0] * src_sum[c] for c in range(3))
                minus = sum_of(rows_now[c][1] * src_im[c] for c in range(3))
                plus = sum_of(rows_now[c][2] * src_re[c] for c in range(3))
                part_re.append((common - minus).astype(jnp.bfloat16).astype(jnp.float32))
                part_im.append((common + plus).astype(jnp.bfloat16).astype(jnp.float32))
            part_sum = [part_re[c] + part_im[c] for c in range(3)]
            for a in range(BLK):
                lead = []
                for c in range(3):
                    at = 3 * (c * BLK + a)
                    lead.append([lead_rows[at + n : at + n + 1, lanes] for n in range(3)])
                for one, two, out in epsilon_cycles:
                    common = lead[one][0] * part_sum[two] - lead[two][0] * part_sum[one]
                    prod_re = common - (lead[one][1] * part_im[two] - lead[two][1] * part_im[one])
                    prod_im = common + (lead[one][2] * part_re[two] - lead[two][2] * part_re[one])
                    where = slice(out * SITES, (out + 1) * SITES)
                    at_re = pl.multiple_of(a * count + first, ROWS)
                    at_im = pl.multiple_of((BLK + a) * count + first, ROWS)
                    prod_ref[pl.ds(at_re, ROWS), where] = prod_re.astype(jnp.bfloat16)
                    prod_ref[pl.ds(at_im, ROWS), where] = prod_im.astype(jnp.bfloat16)
            return carry

        lax.fori_loop(0, count // ROWS, rows_step, 0)


def write_out(acc_ref, last_ref, last_weights, out_ref, count, nev, norm_factor):
    half = BLK * count
    for a in range(BLK):
        at_re = slice(a * count, (a + 1) * count)
        at_im = slice(half + a * count, half + (a + 1) * count)
        rows_re = acc_ref[at_re] + dot_rows(last_ref[at_re], last_weights[...])
        rows_im = acc_ref[at_im] + dot_rows(last_ref[at_im], last_weights[...])
        out_re = (rows_re[:, :nev] - rows_im[:, nev:]) * norm_factor
        out_im = (rows_re[:, nev:] + rows_im[:, :nev]) * norm_factor
        for g in range(count // 8):
            out_ref[g, a] = out_re[g * 8 : g * 8 + 8]
            out_ref[g, BLK + a] = out_im[g * 8 : g * 8 + 8]


def shift_sources(second, vec_ref, src_ref):
    nev, sites = vec_ref.shape[3:]
    lane = lax.broadcasted_iota(jnp.int32, (ROWS, sites), 1)

    def rows_step(i, carry):
        rows = pl.ds(pl.multiple_of(i * ROWS, ROWS), ROWS)
        for r in range(2):
            for c in range(3):
                now = vec_ref[0, r, c, rows].astype(jnp.float32)
                if second:
                    moved = pltpu.roll(now, sites - LZ, 1)
                else:
                    moved = jnp.where(
                        lane % LZ == LZ - 1,
                        pltpu.roll(now, LZ - 1, 1),
                        pltpu.roll(now, sites - 1, 1),
                    )
                src_ref[r, c, rows] = moved
        return carry

    lax.fori_loop(0, nev // ROWS, rows_step, 0)


def sums_kernel(place, extent, norm_factor, order, directions, offsets, momentum, vec_ref, link_ref, *refs):
    nev, sites = vec_ref.shape[3:]
    now = order[place]
    if len(refs) == 9:
        src_ref, out_ref, wide_ref, link_rows, lead_rows, weights, prod_a, prod_b, acc_ref = refs
        count = src_ref.shape[3]

        def source_at(r, c, first, lanes):
            return src_ref[0, r, c, pl.ds(first, ROWS), lanes].astype(jnp.float32)
    else:
        out_ref, wide_ref, link_rows, lead_rows, weights, prod_a, prod_b, acc_ref, moved_ref, _ = refs
        count = nev

        def source_at(r, c, first, lanes):
            return moved_ref[r, c, pl.ds(first, ROWS), lanes]

        @pl.when(directions[now] == 1)
        def _():
            shift_sources(True, vec_ref, moved_ref)

        @pl.when(directions[now] != 1)
        def _():
            shift_sources(False, vec_ref, moved_ref)

    stage_rows(extent, offsets[now], momentum, vec_ref, link_ref, wide_ref, link_rows, lead_rows, weights)
    sums_of(source_at, count, sites, link_rows, lead_rows, weights, (prod_a, prod_b), acc_ref)
    parts = sites // SITES
    write_out(acc_ref, (prod_a, prod_b)[(parts - 1) % 2], weights.at[parts - 1], out_ref, count, nev, norm_factor)


def slice_sums(scalars, vectors, links, source, place, extent, norm_factor):
    _, _, _, nev, sites = vectors.shape
    parts = sites // SITES
    count = nev if source is None else source.shape[3]
    operands = [vectors, links] + ([] if source is None else [source])
    in_specs = [
        pl.BlockSpec((1, 2, 3, nev, sites), lambda i, order, *_: (order[place], 0, 0, 0, 0)),
        pl.BlockSpec(
            (1, 1, 3, 3, 2, sites),
            lambda i, order, directions, *_: (order[place], directions[order[place]], 0, 0, 0, 0),
        ),
    ]
    scratch = [
        pltpu.VMEM((2, 32, sites), jnp.float32),
        pltpu.VMEM((27, sites), jnp.float32),
        pltpu.VMEM((9 * BLK, sites), jnp.float32),
        pltpu.VMEM((parts, 2 * nev, 3 * SITES), jnp.bfloat16),
        pltpu.VMEM((2 * BLK * count, 3 * SITES), jnp.bfloat16),
        pltpu.VMEM((2 * BLK * count, 3 * SITES), jnp.bfloat16),
        pltpu.VMEM((2 * BLK * count, 2 * nev), jnp.float32),
    ]
    if source is None:
        scratch += [pltpu.VMEM((2, 3, nev, sites), jnp.float32), pltpu.VMEM((8, 128), jnp.float32)]
    else:
        in_specs.append(pl.BlockSpec((1, 2, 3, count, sites), lambda i, *_: (0, 0, 0, 0, 0)))
    return pl.pallas_call(
        functools.partial(sums_kernel, place, extent, norm_factor),
        out_shape=jax.ShapeDtypeStruct((count // 8, 2 * BLK, 8, nev), jnp.float32),
        grid_spec=pltpu.PrefetchScalarGridSpec(
            num_scalar_prefetch=4,
            grid=(1,),
            in_specs=in_specs,
            out_specs=pl.BlockSpec((count // 8, 2 * BLK, 8, nev), lambda i, *_: (0, 0, 0, 0)),
            scratch_shapes=scratch,
        ),
        compiler_params=pltpu.CompilerParams(vmem_limit_bytes=40 * 2**20),
        cost_estimate=pl.CostEstimate(
            flops=100 * 2 * BLK * count * 3 * sites, bytes_accessed=2 * 2**20, transcendentals=0
        ),
        name="inner_sums" if source is None else "outer_sums",
    )(*scalars, *operands)


def scatter_kernel(groups, count, *refs):
    parts, out_ref = refs[:count], refs[count]
    send_one, send_two, send_three, recv_one, recv_two, recv_three, sum_one, sems_out, sems_in = refs[count + 1 :]
    me = lax.axis_index("space")
    core = me % 2
    row = (me // 2) % 2
    group = me // 4
    pair = me + 1 - 2 * core
    across = me + 2 - 4 * row
    others = [(group + step) % groups for step in range(1, groups)]
    partners = [other * 4 + row * 2 + core for other in others]
    barrier = pltpu.get_barrier_semaphore()
    for partner in [pair, across] + partners:
        pl.semaphore_signal(barrier, inc=1, device_id={"space": partner}, device_id_type=MESH)
    pl.semaphore_wait(barrier, groups + 1)

    def start(source, target, number, partner):
        copy = pltpu.make_async_remote_copy(
            src_ref=source, dst_ref=target, send_sem=sems_out.at[number], recv_sem=sems_in.at[number],
            device_id={"space": partner}, device_id_type=MESH,
        )
        copy.start()
        return copy

    first = []
    for number, y in enumerate((1 - row, row)):
        for z in range(groups):
            for t in range(count):
                send_one[y, z, t] = parts[t][z, y, 1 - core].astype(jnp.bfloat16)
        first.append(start(send_one.at[y], recv_one.at[y], number, pair))
    first[0].wait()
    second = []
    for number, z in enumerate(others + [group]):
        for t in range(count):
            got = parts[t][z, 1 - row, core] + recv_one[1 - row, z, t].astype(jnp.float32)
            send_two[z, t] = got.astype(jnp.bfloat16)
        second.append(start(send_two.at[z], recv_two.at[z], 2 + number, across))
    first[1].wait()
    for z in range(groups):
        for t in range(count):
            sum_one[z, t] = parts[t][z, row, core] + recv_one[row, z, t].astype(jnp.float32)
    third = []
    for number, other in enumerate(others):
        second[number].wait()
        send_three[other] = (sum_one[other] + recv_two[other].astype(jnp.float32)).astype(jnp.bfloat16)
        third.append(start(send_three.at[other], recv_three.at[number], 2 + groups + number, partners[number]))
    second[-1].wait()
    total = sum_one[group] + recv_two[group].astype(jnp.float32)
    for number in range(groups - 1):
        third[number].wait()
        total = total + recv_three[number].astype(jnp.float32)
    out_ref[...] = total


def scatter_sum(parts, number):
    count = len(parts)
    devices, rows, columns = parts[0].shape
    groups = devices // 4
    whole = pl.BlockSpec(memory_space=pltpu.VMEM)
    bf16 = jnp.bfloat16
    return pl.pallas_call(
        functools.partial(scatter_kernel, groups, count),
        out_shape=jax.ShapeDtypeStruct((count, rows, columns), jnp.float32),
        in_specs=[whole] * count,
        out_specs=whole,
        scratch_shapes=[
            pltpu.VMEM((2, groups, count, rows, columns), bf16),
            pltpu.VMEM((groups, count, rows, columns), bf16),
            pltpu.VMEM((groups, count, rows, columns), bf16),
            pltpu.VMEM((2, groups, count, rows, columns), bf16),
            pltpu.VMEM((groups, count, rows, columns), bf16),
            pltpu.VMEM((groups, count, rows, columns), bf16),
            pltpu.VMEM((groups, count, rows, columns), jnp.float32),
            pltpu.SemaphoreType.DMA((2 * groups + 1,)),
            pltpu.SemaphoreType.DMA((2 * groups + 1,)),
        ],
        compiler_params=pltpu.CompilerParams(
            collective_id=number, has_side_effects=True, vmem_limit_bytes=40 * 2**20
        ),
        name="scatter_sum",
    )(*[part.reshape(groups, 2, 2, rows, columns) for part in parts])


def by_owner(part, devices):
    slices, tiles, parts, eight, nev = part.shape
    own = tiles * eight // devices
    if own == eight:
        moved = jnp.transpose(part, (1, 0, 2, 3, 4))
    else:
        flat = jnp.transpose(part, (0, 2, 1, 3, 4)).reshape(slices, parts, devices, own, nev)
        moved = jnp.transpose(flat, (2, 0, 1, 3, 4))
    return moved.reshape(devices, slices * parts * own, nev)


def on_device(eigenvectors, link_field, momentum, directions, offsets):
    devices = lax.axis_size("space")
    slices, _, _, nev, planes, sites = eigenvectors.shape
    extent_x = planes * devices
    norm_factor = 1.0 / math.sqrt(extent_x * LY * LZ)
    vectors = eigenvectors.reshape(slices, 2, 3, nev, sites)

    inner = (directions != 0).astype(jnp.int32)
    numbers = jnp.arange(slices, dtype=jnp.int32)
    before = (inner[None] < inner[:, None]) | (
        (inner[None] == inner[:, None]) & (numbers[None] < numbers[:, None])
    )
    rank = jnp.sum(before.astype(jnp.int32), axis=1)
    order = jnp.sum(jnp.where(rank[None] == numbers[:, None], numbers[None], 0), axis=1)
    half = slices // 2

    pairs = [(source, (source - 1) % devices) for source in range(devices)]
    chosen = [lax.dynamic_slice_in_dim(vectors, order[place], 1, 0) for place in range(half)]
    chosen, order = lax.optimization_barrier((chosen, order))
    above = [lax.ppermute(plane, "space", pairs) for plane in chosen]

    links = jnp.transpose(
        link_field.reshape(slices, 3, 2, 3, 3, sites), (0, 1, 3, 4, 2, 5)
    )
    scalars = (order, directions, offsets, momentum)
    sums_at = functools.partial(slice_sums, scalars, vectors, links, extent=extent_x, norm_factor=norm_factor)
    inner_sum = scatter_sum([by_owner(sums_at(None, place)[None], devices) for place in range(half, slices)], 0)
    outer_sum = scatter_sum([by_owner(sums_at(above[place], place)[None], devices) for place in range(half)], 1)

    own = nev // devices
    both = jnp.concatenate([outer_sum, inner_sum]).reshape(slices, 2, BLK, own, nev)
    return jnp.take(both, rank, axis=0, mode="clip")


def solution(mesh):
    placed = (
        P("cfg", None, None, None, "space", None),
        P("cfg", None, None, None, None, "space", None),
        P(),
        P(),
        P(),
    )
    return jax.shard_map(
        on_device,
        mesh=mesh,
        in_specs=placed,
        out_specs=P("cfg", None, None, "space", None),
        check_vma=False,
    )
```

```python
import functools
import math

import jax
import jax.numpy as jnp
from jax import lax
from jax.experimental import pallas as pl
from jax.experimental.pallas import tpu as pltpu
from jax.sharding import PartitionSpec as P

BLK = 4
LY = 32
LZ = 32
SITES = 256
ROWS = 16
MESH = pl.DeviceIdType.MESH

epsilon_cycles = ((0, 1, 2), (1, 2, 0), (2, 0, 1))


def phase_row(momentum, x_site, extent, sites):
    site = lax.broadcasted_iota(jnp.int32, (1, sites), 1)
    x_turn = lax.rem(lax.rem(momentum[0] * x_site, extent) + extent, extent)
    y_turns = lax.rem(lax.rem(momentum[1] * (site // LZ), LY) + LY, LY).astype(jnp.float32) / LY
    z_turns = lax.rem(lax.rem(momentum[2] * (site % LZ), LZ) + LZ, LZ).astype(jnp.float32) / LZ
    angles = -2.0 * math.pi * (x_turn.astype(jnp.float32) / extent + y_turns + z_turns)
    return jnp.cos(angles), jnp.sin(angles)


def stage_rows(extent, offset, momentum, vec_ref, link_ref, wide_ref, link_rows, lead_rows, weights):
    nev, sites = vec_ref.shape[3:]
    for row in range(3):
        for column in range(3):
            at = 3 * (3 * row + column)
            pair = link_ref[0, 0, row, column].astype(jnp.float32)
            link_rows[at : at + 1] = pair[0:1]
            link_rows[at + 1 : at + 2] = pair[0:1] + pair[1:2]
            link_rows[at + 2 : at + 3] = pair[1:2] - pair[0:1]
    cosine, sine = phase_row(momentum, lax.axis_index("space"), extent, sites)
    base = pl.multiple_of(jnp.minimum((offset // 16) * 16, nev - 32), 16)
    for c in range(3):
        for r in range(2):
            wide_ref[r] = vec_ref[0, r, c, pl.ds(base, 32)].astype(jnp.float32)
        for a in range(BLK):
            now_re = wide_ref[0, pl.ds(offset - base + a, 1)]
            now_im = wide_ref[1, pl.ds(offset - base + a, 1)]
            at = 3 * (c * BLK + a)
            turned_re = now_re * cosine - now_im * sine
            turned_im = now_re * sine + now_im * cosine
            lead_rows[at : at + 1] = turned_re
            lead_rows[at + 1 : at + 2] = turned_re + turned_im
            lead_rows[at + 2 : at + 3] = turned_im - turned_re
    for part in range(sites // SITES):
        for r in range(2):
            for k in range(3):
                weights[part, r * nev : (r + 1) * nev, k * SITES : (k + 1) * SITES] = vec_ref[
                    0, r, k, :, part * SITES : (part + 1) * SITES
                ]


def sum_of(terms):
    return functools.reduce(lambda left, right: left + right, terms)


def dot_rows(left, right):
    return lax.dot_general(left, right, (((1,), (1,)), ((), ())), preferred_element_type=jnp.float32)


def sums_of(source_at, count, sites, link_rows, lead_rows, weights, prods, acc_ref):
    share = 2 * BLK * ROWS

    for part in range(sites // SITES):
        lanes = slice(part * SITES, (part + 1) * SITES)
        prod_ref = prods[part % 2]
        last_ref = prods[(part + 1) % 2]

        def rows_step(step, carry, part=part, lanes=lanes, prod_ref=prod_ref, last_ref=last_ref):
            if part > 0:
                rows = pl.ds(pl.multiple_of(step * share, share), share)
                now = dot_rows(last_ref[rows], weights[part - 1])
                acc_ref[rows] = now if part == 1 else acc_ref[rows] + now
            first = pl.multiple_of(step * ROWS, ROWS)
            src_re = [source_at(0, c, first, lanes) for c in range(3)]
            src_im = [source_at(1, c, first, lanes) for c in range(3)]
            src_sum = [src_re[c] + src_im[c] for c in range(3)]
            part_re = []
            part_im = []
            for row in range(3):
                rows_now = [
                    [link_rows[at + n : at + n + 1, lanes] for n in range(3)]
                    for at in (9 * row, 9 * row + 3, 9 * row + 6)
                ]
                common = sum_of(rows_now[c][0] * src_sum[c] for c in range(3))
                minus = sum_of(rows_now[c][1] * src_im[c] for c in range(3))
                plus = sum_of(rows_now[c][2] * src_re[c] for c in range(3))
                part_re.append((common - minus).astype(jnp.bfloat16).astype(jnp.float32))
                part_im.append((common + plus).astype(jnp.bfloat16).astype(jnp.float32))
            part_sum = [part_re[c] + part_im[c] for c in range(3)]
            for a in range(BLK):
                lead = []
                for c in range(3):
                    at = 3 * (c * BLK + a)
                    lead.append([lead_rows[at + n : at + n + 1, lanes] for n in range(3)])
                for one, two, out in epsilon_cycles:
                    common = lead[one][0] * part_sum[two] - lead[two][0] * part_sum[one]
                    prod_re = common - (lead[one][1] * part_im[two] - lead[two][1] * part_im[one])
                    prod_im = common + (lead[one][2] * part_re[two] - lead[two][2] * part_re[one])
                    where = slice(out * SITES, (out + 1) * SITES)
                    at_re = pl.multiple_of(a * count + first, ROWS)
                    at_im = pl.multiple_of((BLK + a) * count + first, ROWS)
                    prod_ref[pl.ds(at_re, ROWS), where] = prod_re.astype(jnp.bfloat16)
                    prod_ref[pl.ds(at_im, ROWS), where] = prod_im.astype(jnp.bfloat16)
            return carry

        lax.fori_loop(0, count // ROWS, rows_step, 0)


def write_out(acc_ref, last_ref, last_weights, out_ref, count, nev, norm_factor):
    half = BLK * count
    for a in range(BLK):
        at_re = slice(a * count, (a + 1) * count)
        at_im = slice(half + a * count, half + (a + 1) * count)
        rows_re = acc_ref[at_re] + dot_rows(last_ref[at_re], last_weights[...])
        rows_im = acc_ref[at_im] + dot_rows(last_ref[at_im], last_weights[...])
        out_re = (rows_re[:, :nev] - rows_im[:, nev:]) * norm_factor
        out_im = (rows_re[:, nev:] + rows_im[:, :nev]) * norm_factor
        for g in range(count // 8):
            out_ref[g, a] = out_re[g * 8 : g * 8 + 8]
            out_ref[g, BLK + a] = out_im[g * 8 : g * 8 + 8]


def shift_sources(second, vec_ref, src_ref):
    nev, sites = vec_ref.shape[3:]
    lane = lax.broadcasted_iota(jnp.int32, (ROWS, sites), 1)

    def rows_step(i, carry):
        rows = pl.ds(pl.multiple_of(i * ROWS, ROWS), ROWS)
        for r in range(2):
            for c in range(3):
                now = vec_ref[0, r, c, rows].astype(jnp.float32)
                if second:
                    moved = pltpu.roll(now, sites - LZ, 1)
                else:
                    moved = jnp.where(
                        lane % LZ == LZ - 1,
                        pltpu.roll(now, LZ - 1, 1),
                        pltpu.roll(now, sites - 1, 1),
                    )
                src_ref[r, c, rows] = moved
        return carry

    lax.fori_loop(0, nev // ROWS, rows_step, 0)


def slice_at(directions, place):
    slices = directions.shape[0]
    inner = [jnp.where(directions[t] != 0, 1, 0) for t in range(slices)]
    outer_count = slices - sum_of(inner)
    seen_outer = 0
    seen_inner = outer_count
    found = 0
    for t in range(slices):
        rank = jnp.where(inner[t] == 0, seen_outer, seen_inner)
        found = found + jnp.where(rank == place, t, 0)
        seen_outer = seen_outer + 1 - inner[t]
        seen_inner = seen_inner + inner[t]
    return found


def choose_kernel(directions, vec_ref, *refs):
    outs, sems = refs[:-1], refs[-1]
    copies = []
    for place, out_ref in enumerate(outs):
        now = slice_at(directions, place)
        copies.append(pltpu.make_async_copy(vec_ref.at[pl.ds(now, 1)], out_ref, sems.at[place]))
        copies[-1].start()
    for copy in copies:
        copy.wait()


def choose_planes(directions, vectors, count):
    anywhere = pl.BlockSpec(memory_space=pl.ANY)
    return pl.pallas_call(
        choose_kernel,
        out_shape=[jax.ShapeDtypeStruct((1,) + vectors.shape[1:], vectors.dtype)] * count,
        grid_spec=pltpu.PrefetchScalarGridSpec(
            num_scalar_prefetch=1,
            grid=(1,),
            in_specs=[anywhere],
            out_specs=[anywhere] * count,
            scratch_shapes=[pltpu.SemaphoreType.DMA((count,))],
        ),
        compiler_params=pltpu.CompilerParams(vmem_limit_bytes=56 * 2**20),
        name="choose_planes",
    )(directions, vectors)


def sums_kernel(place, extent, norm_factor, directions, offsets, momentum, vec_ref, link_ref, *refs):
    nev, sites = vec_ref.shape[3:]
    now = slice_at(directions, place)
    if len(refs) == 9:
        src_ref, out_ref, wide_ref, link_rows, lead_rows, weights, prod_a, prod_b, acc_ref = refs
        count = src_ref.shape[3]

        def source_at(r, c, first, lanes):
            return src_ref[0, r, c, pl.ds(first, ROWS), lanes].astype(jnp.float32)
    else:
        out_ref, wide_ref, link_rows, lead_rows, weights, prod_a, prod_b, acc_ref, moved_ref, _ = refs
        count = nev

        def source_at(r, c, first, lanes):
            return moved_ref[r, c, pl.ds(first, ROWS), lanes]

        @pl.when(directions[now] == 1)
        def _():
            shift_sources(True, vec_ref, moved_ref)

        @pl.when(directions[now] != 1)
        def _():
            shift_sources(False, vec_ref, moved_ref)

    stage_rows(extent, offsets[now], momentum, vec_ref, link_ref, wide_ref, link_rows, lead_rows, weights)
    sums_of(source_at, count, sites, link_rows, lead_rows, weights, (prod_a, prod_b), acc_ref)
    parts = sites // SITES
    write_out(acc_ref, (prod_a, prod_b)[(parts - 1) % 2], weights.at[parts - 1], out_ref, count, nev, norm_factor)


def slice_sums(scalars, vectors, links, source, place, extent, norm_factor):
    _, _, _, nev, sites = vectors.shape
    parts = sites // SITES
    count = nev if source is None else source.shape[3]
    operands = [vectors, links] + ([] if source is None else [source])
    in_specs = [
        pl.BlockSpec((1, 2, 3, nev, sites), lambda i, directions, *_: (slice_at(directions, place), 0, 0, 0, 0)),
        pl.BlockSpec(
            (1, 1, 3, 3, 2, sites),
            lambda i, directions, *_: (
                slice_at(directions, place), directions[slice_at(directions, place)], 0, 0, 0, 0
            ),
        ),
    ]
    scratch = [
        pltpu.VMEM((2, 32, sites), jnp.float32),
        pltpu.VMEM((27, sites), jnp.float32),
        pltpu.VMEM((9 * BLK, sites), jnp.float32),
        pltpu.VMEM((parts, 2 * nev, 3 * SITES), jnp.bfloat16),
        pltpu.VMEM((2 * BLK * count, 3 * SITES), jnp.bfloat16),
        pltpu.VMEM((2 * BLK * count, 3 * SITES), jnp.bfloat16),
        pltpu.VMEM((2 * BLK * count, 2 * nev), jnp.float32),
    ]
    if source is None:
        scratch += [pltpu.VMEM((2, 3, nev, sites), jnp.float32), pltpu.VMEM((8, 128), jnp.float32)]
    else:
        in_specs.append(pl.BlockSpec((1, 2, 3, count, sites), lambda i, *_: (0, 0, 0, 0, 0)))
    return pl.pallas_call(
        functools.partial(sums_kernel, place, extent, norm_factor),
        out_shape=jax.ShapeDtypeStruct((count // 8, 2 * BLK, 8, nev), jnp.float32),
        grid_spec=pltpu.PrefetchScalarGridSpec(
            num_scalar_prefetch=3,
            grid=(1,),
            in_specs=in_specs,
            out_specs=pl.BlockSpec((count // 8, 2 * BLK, 8, nev), lambda i, *_: (0, 0, 0, 0)),
            scratch_shapes=scratch,
        ),
        compiler_params=pltpu.CompilerParams(vmem_limit_bytes=40 * 2**20),
        cost_estimate=pl.CostEstimate(
            flops=100 * 2 * BLK * count * 3 * sites, bytes_accessed=2 * 2**20, transcendentals=0
        ),
        name="inner_sums" if source is None else "outer_sums",
    )(*scalars, *operands)


def scatter_kernel(groups, count, *refs):
    parts, out_ref = refs[:count], refs[count]
    send_one, send_two, send_three, recv_one, recv_two, recv_three, sum_one, sems_out, sems_in = refs[count + 1 :]
    me = lax.axis_index("space")
    core = me % 2
    row = (me // 2) % 2
    group = me // 4
    pair = me + 1 - 2 * core
    across = me + 2 - 4 * row
    others = [(group + step) % groups for step in range(1, groups)]
    partners = [other * 4 + row * 2 + core for other in others]
    barrier = pltpu.get_barrier_semaphore()
    for partner in [pair, across] + partners:
        pl.semaphore_signal(barrier, inc=1, device_id={"space": partner}, device_id_type=MESH)
    pl.semaphore_wait(barrier, groups + 1)

    def start(source, target, number, partner):
        copy = pltpu.make_async_remote_copy(
            src_ref=source, dst_ref=target, send_sem=sems_out.at[number], recv_sem=sems_in.at[number],
            device_id={"space": partner}, device_id_type=MESH,
        )
        copy.start()
        return copy

    first = []
    for number, y in enumerate((1 - row, row)):
        for z in range(groups):
            for t in range(count):
                send_one[y, z, t] = parts[t][z, y, 1 - core].astype(jnp.bfloat16)
        first.append(start(send_one.at[y], recv_one.at[y], number, pair))
    first[0].wait()
    second = []
    for number, z in enumerate(others + [group]):
        for t in range(count):
            got = parts[t][z, 1 - row, core] + recv_one[1 - row, z, t].astype(jnp.float32)
            send_two[z, t] = got.astype(jnp.bfloat16)
        second.append(start(send_two.at[z], recv_two.at[z], 2 + number, across))
    first[1].wait()
    for z in range(groups):
        for t in range(count):
            sum_one[z, t] = parts[t][z, row, core] + recv_one[row, z, t].astype(jnp.float32)
    third = []
    for number, other in enumerate(others):
        second[number].wait()
        send_three[other] = (sum_one[other] + recv_two[other].astype(jnp.float32)).astype(jnp.bfloat16)
        third.append(start(send_three.at[other], recv_three.at[number], 2 + groups + number, partners[number]))
    second[-1].wait()
    total = sum_one[group] + recv_two[group].astype(jnp.float32)
    for number in range(groups - 1):
        third[number].wait()
        total = total + recv_three[number].astype(jnp.float32)
    out_ref[...] = total


def scatter_sum(parts, number):
    count = len(parts)
    devices, rows, columns = parts[0].shape
    groups = devices // 4
    whole = pl.BlockSpec(memory_space=pltpu.VMEM)
    bf16 = jnp.bfloat16
    return pl.pallas_call(
        functools.partial(scatter_kernel, groups, count),
        out_shape=jax.ShapeDtypeStruct((count, rows, columns), jnp.float32),
        in_specs=[whole] * count,
        out_specs=whole,
        scratch_shapes=[
            pltpu.VMEM((2, groups, count, rows, columns), bf16),
            pltpu.VMEM((groups, count, rows, columns), bf16),
            pltpu.VMEM((groups, count, rows, columns), bf16),
            pltpu.VMEM((2, groups, count, rows, columns), bf16),
            pltpu.VMEM((groups, count, rows, columns), bf16),
            pltpu.VMEM((groups, count, rows, columns), bf16),
            pltpu.VMEM((groups, count, rows, columns), jnp.float32),
            pltpu.SemaphoreType.DMA((2 * groups + 1,)),
            pltpu.SemaphoreType.DMA((2 * groups + 1,)),
        ],
        compiler_params=pltpu.CompilerParams(
            collective_id=number, has_side_effects=True, vmem_limit_bytes=40 * 2**20
        ),
        name="scatter_sum",
    )(*[part.reshape(groups, 2, 2, rows, columns) for part in parts])


def by_owner(part, devices):
    slices, tiles, parts, eight, nev = part.shape
    own = tiles * eight // devices
    if own == eight:
        moved = jnp.transpose(part, (1, 0, 2, 3, 4))
    else:
        flat = jnp.transpose(part, (0, 2, 1, 3, 4)).reshape(slices, parts, devices, own, nev)
        moved = jnp.transpose(flat, (2, 0, 1, 3, 4))
    return moved.reshape(devices, slices * parts * own, nev)


def on_device(eigenvectors, link_field, momentum, directions, offsets):
    devices = lax.axis_size("space")
    slices, _, _, nev, planes, sites = eigenvectors.shape
    extent_x = planes * devices
    norm_factor = 1.0 / math.sqrt(extent_x * LY * LZ)
    vectors = eigenvectors.reshape(slices, 2, 3, nev, sites)

    inner = (directions != 0).astype(jnp.int32)
    numbers = jnp.arange(slices, dtype=jnp.int32)
    before = (inner[None] < inner[:, None]) | (
        (inner[None] == inner[:, None]) & (numbers[None] < numbers[:, None])
    )
    rank = jnp.sum(before.astype(jnp.int32), axis=1)
    half = slices // 2

    pairs = [(source, (source - 1) % devices) for source in range(devices)]
    chosen = choose_planes(directions, vectors, half)
    chosen, turned = lax.optimization_barrier((chosen, directions))
    above = [lax.ppermute(plane, "space", pairs) for plane in chosen]

    links = jnp.transpose(
        link_field.reshape(slices, 3, 2, 3, 3, sites), (0, 1, 3, 4, 2, 5)
    )
    scalars = (turned, offsets, momentum)
    sums_at = functools.partial(slice_sums, scalars, vectors, links, extent=extent_x, norm_factor=norm_factor)
    inner = [by_owner(sums_at(None, place)[None], devices) for place in range(half, slices)]
    outer = [by_owner(sums_at(above[place], place)[None], devices) for place in range(half)]
    sums = scatter_sum(outer + inner, 0)

    own = nev // devices
    both = sums.reshape(slices, 2, BLK, own, nev)
    return jnp.take(both, rank, axis=0, mode="clip")


def solution(mesh):
    placed = (
        P("cfg", None, None, None, "space", None),
        P("cfg", None, None, None, None, "space", None),
        P(),
        P(),
        P(),
    )
    return jax.shard_map(
        on_device,
        mesh=mesh,
        in_specs=placed,
        out_specs=P("cfg", None, None, "space", None),
        check_vma=False,
    )
```

```python
import functools
import math

import jax
import jax.numpy as jnp
from jax import lax
from jax.experimental import pallas as pl
from jax.experimental.pallas import tpu as pltpu
from jax.sharding import PartitionSpec as P

BLK = 4
LY = 32
LZ = 32
SITES = 256
ROWS = 16
MESH = pl.DeviceIdType.MESH

epsilon_cycles = ((0, 1, 2), (1, 2, 0), (2, 0, 1))


def phase_row(momentum, x_site, extent, sites):
    site = lax.broadcasted_iota(jnp.int32, (1, sites), 1)
    x_turn = lax.rem(lax.rem(momentum[0] * x_site, extent) + extent, extent)
    y_turns = lax.rem(lax.rem(momentum[1] * (site // LZ), LY) + LY, LY).astype(jnp.float32) / LY
    z_turns = lax.rem(lax.rem(momentum[2] * (site % LZ), LZ) + LZ, LZ).astype(jnp.float32) / LZ
    angles = -2.0 * math.pi * (x_turn.astype(jnp.float32) / extent + y_turns + z_turns)
    return jnp.cos(angles), jnp.sin(angles)


def stage_rows(extent, offset, momentum, vec_ref, link_ref, wide_ref, link_rows, lead_rows, weights):
    nev, sites = vec_ref.shape[3:]
    for row in range(3):
        for column in range(3):
            at = 3 * (3 * row + column)
            pair = link_ref[0, 0, row, column].astype(jnp.float32)
            link_rows[at : at + 1] = pair[0:1]
            link_rows[at + 1 : at + 2] = pair[0:1] + pair[1:2]
            link_rows[at + 2 : at + 3] = pair[1:2] - pair[0:1]
    cosine, sine = phase_row(momentum, lax.axis_index("space"), extent, sites)
    base = pl.multiple_of(jnp.minimum((offset // 16) * 16, nev - 32), 16)
    for c in range(3):
        for r in range(2):
            wide_ref[r] = vec_ref[0, r, c, pl.ds(base, 32)].astype(jnp.float32)
        for a in range(BLK):
            now_re = wide_ref[0, pl.ds(offset - base + a, 1)]
            now_im = wide_ref[1, pl.ds(offset - base + a, 1)]
            at = 3 * (c * BLK + a)
            turned_re = now_re * cosine - now_im * sine
            turned_im = now_re * sine + now_im * cosine
            lead_rows[at : at + 1] = turned_re
            lead_rows[at + 1 : at + 2] = turned_re + turned_im
            lead_rows[at + 2 : at + 3] = turned_im - turned_re
    for part in range(sites // SITES):
        for r in range(2):
            for k in range(3):
                weights[part, r * nev : (r + 1) * nev, k * SITES : (k + 1) * SITES] = vec_ref[
                    0, r, k, :, part * SITES : (part + 1) * SITES
                ]


def sum_of(terms):
    return functools.reduce(lambda left, right: left + right, terms)


def dot_rows(left, right):
    return lax.dot_general(left, right, (((1,), (1,)), ((), ())), preferred_element_type=jnp.float32)


def sums_of(source_at, count, sites, link_rows, lead_rows, weights, prods, acc_ref):
    share = 2 * BLK * ROWS

    for part in range(sites // SITES):
        lanes = slice(part * SITES, (part + 1) * SITES)
        prod_ref = prods[part % 2]
        last_ref = prods[(part + 1) % 2]

        def rows_step(step, carry, part=part, lanes=lanes, prod_ref=prod_ref, last_ref=last_ref):
            if part > 0:
                rows = pl.ds(pl.multiple_of(step * share, share), share)
                now = dot_rows(last_ref[rows], weights[part - 1])
                acc_ref[rows] = now if part == 1 else acc_ref[rows] + now
            first = pl.multiple_of(step * ROWS, ROWS)
            src_re = [source_at(0, c, first, lanes) for c in range(3)]
            src_im = [source_at(1, c, first, lanes) for c in range(3)]
            src_sum = [src_re[c] + src_im[c] for c in range(3)]
            part_re = []
            part_im = []
            for row in range(3):
                rows_now = [
                    [link_rows[at + n : at + n + 1, lanes] for n in range(3)]
                    for at in (9 * row, 9 * row + 3, 9 * row + 6)
                ]
                common = sum_of(rows_now[c][0] * src_sum[c] for c in range(3))
                minus = sum_of(rows_now[c][1] * src_im[c] for c in range(3))
                plus = sum_of(rows_now[c][2] * src_re[c] for c in range(3))
                part_re.append((common - minus).astype(jnp.bfloat16).astype(jnp.float32))
                part_im.append((common + plus).astype(jnp.bfloat16).astype(jnp.float32))
            part_sum = [part_re[c] + part_im[c] for c in range(3)]
            for a in range(BLK):
                lead = []
                for c in range(3):
                    at = 3 * (c * BLK + a)
                    lead.append([lead_rows[at + n : at + n + 1, lanes] for n in range(3)])
                for one, two, out in epsilon_cycles:
                    common = lead[one][0] * part_sum[two] - lead[two][0] * part_sum[one]
                    prod_re = common - (lead[one][1] * part_im[two] - lead[two][1] * part_im[one])
                    prod_im = common + (lead[one][2] * part_re[two] - lead[two][2] * part_re[one])
                    where = slice(out * SITES, (out + 1) * SITES)
                    at_re = pl.multiple_of(a * count + first, ROWS)
                    at_im = pl.multiple_of((BLK + a) * count + first, ROWS)
                    prod_ref[pl.ds(at_re, ROWS), where] = prod_re.astype(jnp.bfloat16)
                    prod_ref[pl.ds(at_im, ROWS), where] = prod_im.astype(jnp.bfloat16)
            return carry

        lax.fori_loop(0, count // ROWS, rows_step, 0)


def write_out(acc_ref, last_ref, last_weights, out_ref, count, nev, norm_factor):
    half = BLK * count
    for a in range(BLK):
        at_re = slice(a * count, (a + 1) * count)
        at_im = slice(half + a * count, half + (a + 1) * count)
        rows_re = acc_ref[at_re] + dot_rows(last_ref[at_re], last_weights[...])
        rows_im = acc_ref[at_im] + dot_rows(last_ref[at_im], last_weights[...])
        out_re = (rows_re[:, :nev] - rows_im[:, nev:]) * norm_factor
        out_im = (rows_re[:, nev:] + rows_im[:, :nev]) * norm_factor
        for g in range(count // 8):
            out_ref[g, a] = out_re[g * 8 : g * 8 + 8]
            out_ref[g, BLK + a] = out_im[g * 8 : g * 8 + 8]


def shift_sources(second, vec_ref, src_ref):
    nev, sites = vec_ref.shape[3:]
    lane = lax.broadcasted_iota(jnp.int32, (ROWS, sites), 1)

    def rows_step(i, carry):
        rows = pl.ds(pl.multiple_of(i * ROWS, ROWS), ROWS)
        for r in range(2):
            for c in range(3):
                now = vec_ref[0, r, c, rows].astype(jnp.float32)
                if second:
                    moved = pltpu.roll(now, sites - LZ, 1)
                else:
                    moved = jnp.where(
                        lane % LZ == LZ - 1,
                        pltpu.roll(now, LZ - 1, 1),
                        pltpu.roll(now, sites - 1, 1),
                    )
                src_ref[r, c, rows] = moved
        return carry

    lax.fori_loop(0, nev // ROWS, rows_step, 0)


def slice_at(directions, place):
    slices = directions.shape[0]
    inner = [jnp.where(directions[t] != 0, 1, 0) for t in range(slices)]
    outer_count = slices - sum_of(inner)
    seen_outer = 0
    seen_inner = outer_count
    found = 0
    for t in range(slices):
        rank = jnp.where(inner[t] == 0, seen_outer, seen_inner)
        found = found + jnp.where(rank == place, t, 0)
        seen_outer = seen_outer + 1 - inner[t]
        seen_inner = seen_inner + inner[t]
    return found


def choose_kernel(directions, *refs):
    count = len(refs) // 2
    for place in range(count):
        refs[count + place][...] = refs[place][...]


def choose_planes(directions, vectors, count):
    _, _, colors, nev, sites = vectors.shape

    def block(place):
        return pl.BlockSpec(
            (1, 2, 1, nev, sites), lambda c, directions: (slice_at(directions, place), 0, c, 0, 0)
        )

    return pl.pallas_call(
        choose_kernel,
        out_shape=[jax.ShapeDtypeStruct((1,) + vectors.shape[1:], vectors.dtype)] * count,
        grid_spec=pltpu.PrefetchScalarGridSpec(
            num_scalar_prefetch=1,
            grid=(colors,),
            in_specs=[block(place) for place in range(count)],
            out_specs=[pl.BlockSpec((1, 2, 1, nev, sites), lambda c, directions: (0, 0, c, 0, 0))] * count,
        ),
        compiler_params=pltpu.CompilerParams(vmem_limit_bytes=56 * 2**20),
        name="choose_planes",
    )(directions, *[vectors] * count)


def sums_kernel(place, extent, norm_factor, directions, offsets, momentum, vec_ref, link_ref, *refs):
    nev, sites = vec_ref.shape[3:]
    now = slice_at(directions, place)
    if len(refs) == 9:
        src_ref, out_ref, wide_ref, link_rows, lead_rows, weights, prod_a, prod_b, acc_ref = refs
        count = src_ref.shape[3]

        def source_at(r, c, first, lanes):
            return src_ref[0, r, c, pl.ds(first, ROWS), lanes].astype(jnp.float32)
    else:
        out_ref, wide_ref, link_rows, lead_rows, weights, prod_a, prod_b, acc_ref, moved_ref, _ = refs
        count = nev

        def source_at(r, c, first, lanes):
            return moved_ref[r, c, pl.ds(first, ROWS), lanes]

        @pl.when(directions[now] == 1)
        def _():
            shift_sources(True, vec_ref, moved_ref)

        @pl.when(directions[now] != 1)
        def _():
            shift_sources(False, vec_ref, moved_ref)

    stage_rows(extent, offsets[now], momentum, vec_ref, link_ref, wide_ref, link_rows, lead_rows, weights)
    sums_of(source_at, count, sites, link_rows, lead_rows, weights, (prod_a, prod_b), acc_ref)
    parts = sites // SITES
    write_out(acc_ref, (prod_a, prod_b)[(parts - 1) % 2], weights.at[parts - 1], out_ref, count, nev, norm_factor)


def slice_sums(scalars, vectors, links, source, place, extent, norm_factor):
    _, _, _, nev, sites = vectors.shape
    parts = sites // SITES
    count = nev if source is None else source.shape[3]
    operands = [vectors, links] + ([] if source is None else [source])
    in_specs = [
        pl.BlockSpec((1, 2, 3, nev, sites), lambda i, directions, *_: (slice_at(directions, place), 0, 0, 0, 0)),
        pl.BlockSpec(
            (1, 1, 3, 3, 2, sites),
            lambda i, directions, *_: (
                slice_at(directions, place), directions[slice_at(directions, place)], 0, 0, 0, 0
            ),
        ),
    ]
    scratch = [
        pltpu.VMEM((2, 32, sites), jnp.float32),
        pltpu.VMEM((27, sites), jnp.float32),
        pltpu.VMEM((9 * BLK, sites), jnp.float32),
        pltpu.VMEM((parts, 2 * nev, 3 * SITES), jnp.bfloat16),
        pltpu.VMEM((2 * BLK * count, 3 * SITES), jnp.bfloat16),
        pltpu.VMEM((2 * BLK * count, 3 * SITES), jnp.bfloat16),
        pltpu.VMEM((2 * BLK * count, 2 * nev), jnp.float32),
    ]
    if source is None:
        scratch += [pltpu.VMEM((2, 3, nev, sites), jnp.float32), pltpu.VMEM((8, 128), jnp.float32)]
    else:
        in_specs.append(pl.BlockSpec((1, 2, 3, count, sites), lambda i, *_: (0, 0, 0, 0, 0)))
    return pl.pallas_call(
        functools.partial(sums_kernel, place, extent, norm_factor),
        out_shape=jax.ShapeDtypeStruct((count // 8, 2 * BLK, 8, nev), jnp.float32),
        grid_spec=pltpu.PrefetchScalarGridSpec(
            num_scalar_prefetch=3,
            grid=(1,),
            in_specs=in_specs,
            out_specs=pl.BlockSpec((count // 8, 2 * BLK, 8, nev), lambda i, *_: (0, 0, 0, 0)),
            scratch_shapes=scratch,
        ),
        compiler_params=pltpu.CompilerParams(vmem_limit_bytes=40 * 2**20),
        cost_estimate=pl.CostEstimate(
            flops=100 * 2 * BLK * count * 3 * sites, bytes_accessed=2 * 2**20, transcendentals=0
        ),
        name="inner_sums" if source is None else "outer_sums",
    )(*scalars, *operands)


def scatter_kernel(groups, count, *refs):
    parts, out_ref = refs[:count], refs[count]
    send_one, send_two, send_three, recv_one, recv_two, recv_three, sum_one, sems_out, sems_in = refs[count + 1 :]
    me = lax.axis_index("space")
    core = me % 2
    row = (me // 2) % 2
    group = me // 4
    pair = me + 1 - 2 * core
    across = me + 2 - 4 * row
    others = [(group + step) % groups for step in range(1, groups)]
    partners = [other * 4 + row * 2 + core for other in others]
    barrier = pltpu.get_barrier_semaphore()
    for partner in [pair, across] + partners:
        pl.semaphore_signal(barrier, inc=1, device_id={"space": partner}, device_id_type=MESH)
    pl.semaphore_wait(barrier, groups + 1)

    def start(source, target, number, partner):
        copy = pltpu.make_async_remote_copy(
            src_ref=source, dst_ref=target, send_sem=sems_out.at[number], recv_sem=sems_in.at[number],
            device_id={"space": partner}, device_id_type=MESH,
        )
        copy.start()
        return copy

    first = []
    for number, y in enumerate((1 - row, row)):
        for z in range(groups):
            for t in range(count):
                send_one[y, z, t] = parts[t][z, y, 1 - core].astype(jnp.bfloat16)
        first.append(start(send_one.at[y], recv_one.at[y], number, pair))
    first[0].wait()
    second = []
    for number, z in enumerate(others + [group]):
        for t in range(count):
            got = parts[t][z, 1 - row, core] + recv_one[1 - row, z, t].astype(jnp.float32)
            send_two[z, t] = got.astype(jnp.bfloat16)
        second.append(start(send_two.at[z], recv_two.at[z], 2 + number, across))
    first[1].wait()
    for z in range(groups):
        for t in range(count):
            sum_one[z, t] = parts[t][z, row, core] + recv_one[row, z, t].astype(jnp.float32)
    third = []
    for number, other in enumerate(others):
        second[number].wait()
        send_three[other] = (sum_one[other] + recv_two[other].astype(jnp.float32)).astype(jnp.bfloat16)
        third.append(start(send_three.at[other], recv_three.at[number], 2 + groups + number, partners[number]))
    second[-1].wait()
    total = sum_one[group] + recv_two[group].astype(jnp.float32)
    for number in range(groups - 1):
        third[number].wait()
        total = total + recv_three[number].astype(jnp.float32)
    out_ref[...] = total


def scatter_sum(parts, number):
    count = len(parts)
    devices, rows, columns = parts[0].shape
    groups = devices // 4
    whole = pl.BlockSpec(memory_space=pltpu.VMEM)
    bf16 = jnp.bfloat16
    return pl.pallas_call(
        functools.partial(scatter_kernel, groups, count),
        out_shape=jax.ShapeDtypeStruct((count, rows, columns), jnp.float32),
        in_specs=[whole] * count,
        out_specs=whole,
        scratch_shapes=[
            pltpu.VMEM((2, groups, count, rows, columns), bf16),
            pltpu.VMEM((groups, count, rows, columns), bf16),
            pltpu.VMEM((groups, count, rows, columns), bf16),
            pltpu.VMEM((2, groups, count, rows, columns), bf16),
            pltpu.VMEM((groups, count, rows, columns), bf16),
            pltpu.VMEM((groups, count, rows, columns), bf16),
            pltpu.VMEM((groups, count, rows, columns), jnp.float32),
            pltpu.SemaphoreType.DMA((2 * groups + 1,)),
            pltpu.SemaphoreType.DMA((2 * groups + 1,)),
        ],
        compiler_params=pltpu.CompilerParams(
            collective_id=number, has_side_effects=True, vmem_limit_bytes=40 * 2**20
        ),
        name="scatter_sum",
    )(*[part.reshape(groups, 2, 2, rows, columns) for part in parts])


def by_owner(part, devices):
    slices, tiles, parts, eight, nev = part.shape
    own = tiles * eight // devices
    if own == eight:
        moved = jnp.transpose(part, (1, 0, 2, 3, 4))
    else:
        flat = jnp.transpose(part, (0, 2, 1, 3, 4)).reshape(slices, parts, devices, own, nev)
        moved = jnp.transpose(flat, (2, 0, 1, 3, 4))
    return moved.reshape(devices, slices * parts * own, nev)


def on_device(eigenvectors, link_field, momentum, directions, offsets):
    devices = lax.axis_size("space")
    slices, _, _, nev, planes, sites = eigenvectors.shape
    extent_x = planes * devices
    norm_factor = 1.0 / math.sqrt(extent_x * LY * LZ)
    vectors = eigenvectors.reshape(slices, 2, 3, nev, sites)

    inner = (directions != 0).astype(jnp.int32)
    numbers = jnp.arange(slices, dtype=jnp.int32)
    before = (inner[None] < inner[:, None]) | (
        (inner[None] == inner[:, None]) & (numbers[None] < numbers[:, None])
    )
    rank = jnp.sum(before.astype(jnp.int32), axis=1)
    half = slices // 2

    pairs = [(source, (source - 1) % devices) for source in range(devices)]
    chosen = choose_planes(directions, vectors, half)
    chosen, turned = lax.optimization_barrier((chosen, directions))
    above = [lax.ppermute(plane, "space", pairs) for plane in chosen]

    links = jnp.transpose(
        link_field.reshape(slices, 3, 2, 3, 3, sites), (0, 1, 3, 4, 2, 5)
    )
    scalars = (turned, offsets, momentum)
    sums_at = functools.partial(slice_sums, scalars, vectors, links, extent=extent_x, norm_factor=norm_factor)
    inner = [by_owner(sums_at(None, place)[None], devices) for place in range(half, slices)]
    outer = [by_owner(sums_at(above[place], place)[None], devices) for place in range(half)]
    sums = scatter_sum(outer + inner, 0)

    own = nev // devices
    both = sums.reshape(slices, 2, BLK, own, nev)
    return jnp.take(both, rank, axis=0, mode="clip")


def solution(mesh):
    placed = (
        P("cfg", None, None, None, "space", None),
        P("cfg", None, None, None, None, "space", None),
        P(),
        P(),
        P(),
    )
    return jax.shard_map(
        on_device,
        mesh=mesh,
        in_specs=placed,
        out_specs=P("cfg", None, None, "space", None),
        check_vma=False,
    )
```
